32 devices in a mesh: rows: 16 (over z, y, x), cols: 2 (over core).
Axes of the slice: x: 2, y: 2, z: 4, core: 2. Of those that a mesh axis runs over, the one named last changes fastest.
Arguments:
- momentum_codes: int32 [2, 8192, 8192], P(None, 'rows', 'cols'), may hold values from 0 to 255
- block_amax_scales: float32 [2, 8192, 4], P(None, 'rows'), may hold values from 0.05 to 1
- code_table: float32 [256], replicated, may hold values from -1 to 1
- gradient: bfloat16 [2, 8192, 8192], P(None, 'rows', 'cols'), may hold values from -4 to 4
- weight: bfloat16 [2, 8192, 8192], P(None, 'rows', 'cols'), may hold values from -6 to 6
- right_basis: bfloat16 [2, 8192, 256], P(None, 'cols'), may hold values from -0.0625 to 0.0625
Outputs:
- new_momentum: bfloat16 [2, 8192, 8192], P(None, 'rows', 'cols')
- fresh_block_scales: float32 [2, 8192, 4], P(None, 'rows')
- new_basis: bfloat16 [2, 8192, 256], P(None, 'cols')
- new_weight: bfloat16 [2, 8192, 8192], P(None, 'rows', 'cols')
The draws below stay inside these ranges and needn't reach their ends.
All inputs are finite; a program needn't handle non-finite values.
Results may differ from the reference program's by a relative error of at most 0.005.
Values sent between devices are 32-bit elements; how exact they have to be, the bound alone decides.
A program may use at most 192 MiB of HBM per device.

```python
import math
import jax
import jax.numpy as jnp
from jax import lax

D = 8192
RANK = 256
BLOCK = 2048
LEVELS = 256
MATS = 2
NBLK = 4


def place_ends(drawn, rng, low, high):
    extent = drawn.shape
    index_at = [jax.random.randint(jax.random.fold_in(rng, axis), (), 0, extent[axis]) for axis in range(len(extent))]
    drawn = drawn.at[tuple(index_at)].set(low)
    longest = extent.index(max(extent))
    index_at[longest] = (index_at[longest] + 1) % extent[longest]
    return drawn.at[tuple(index_at)].set(high)


def shard_levels(key, shape, cuts, least, top_value):
    def one(axis_at, shards_of):
        heights = jax.random.uniform(jax.random.fold_in(jax.random.fold_in(key, 6), axis_at), (shards_of,), jnp.float32, least / len(cuts), top_value / len(cuts))
        return jnp.repeat(jnp.exp(heights), shape[axis_at] // shards_of).reshape((-1,) + (1,) * (len(shape) - axis_at - 1))

    factor_of = one(*cuts[0])
    for cut in cuts[1:]:
        factor_of = factor_of * one(*cut)
    return factor_of


def scatter_about(own_key, extent, spread, reach, pieces=(), held_as=jnp.bfloat16):
    values = jax.random.normal(own_key, extent, jnp.float32) * spread
    if len(pieces) > 0:
        values = shard_levels(own_key, extent, pieces, -0.22, 0.18) * values
    return jnp.clip(values, min=-reach, max=reach).astype(held_as)


def setup_inputs(seed: int = 0) -> dict:
    streams_of = jax.random.split(jax.random.key(seed), 7)
    return {
        "momentum_codes": place_ends(jax.random.randint(streams_of[0], (MATS, D, D), 0, LEVELS), jax.random.fold_in(streams_of[0], 1), 0, LEVELS - 1).astype(jnp.int32),
        "block_amax_scales": jnp.clip(jnp.exp(math.log(1.0) - 2.9957323 * jax.random.uniform(streams_of[1], (MATS, D, NBLK), jnp.float32) ** shard_levels(streams_of[1], (MATS, D, NBLK), ((1, 16),), -0.2, 0.2)), 0.05, 1.0),
        "code_table": jnp.clip(jax.random.uniform(streams_of[2], (LEVELS,), jnp.float32, -1.0, 1.0), -1.0, 1.0),
        "gradient": scatter_about(streams_of[3], (MATS, D, D), 0.5, 4.0, ((1, 16), (2, 2))),
        "weight": scatter_about(streams_of[4], (MATS, D, D), 1.0, 6.0, ((1, 16), (2, 2))),
        "right_basis": scatter_about(streams_of[5], (MATS, D, RANK), D ** -0.5, 0.0625, ((1, 2),)),
    }


epsilon = 1e-06
momentum_decay = 0.95
step_size = 0.5

def triangular_solved_rows(cholesky_lower, row_block):
    return jax.scipy.linalg.solve_triangular(cholesky_lower, row_block.T, lower=True).T

def reference(momentum_codes, block_amax_scales, code_table, gradient, weight, right_basis):
    peak_magnitude = lax.Precision.HIGHEST
    values = code_table[momentum_codes]
    scale_columns = jnp.repeat(block_amax_scales, BLOCK, axis=2)
    buffer = values * scale_columns + gradient.astype(jnp.float32)
    power_rows = jnp.einsum('mrn,mnk->mrk', buffer, right_basis.astype(jnp.float32), precision=peak_magnitude)
    basis_gram_product = jnp.einsum('mrk,mrl->mkl', power_rows, power_rows, precision=peak_magnitude)
    cholesky_lower = jnp.linalg.cholesky(basis_gram_product)
    ortho_rows = jax.vmap(triangular_solved_rows)(cholesky_lower, power_rows)
    back_rows = jnp.einsum('mrn,mrk->mnk', buffer, ortho_rows, precision=peak_magnitude)
    square_sums = lax.optimization_barrier(jnp.sum(back_rows * back_rows, axis=1))
    basis_full = back_rows * lax.rsqrt(square_sums + epsilon)[:, None, :]
    residual = buffer - (1.0 - momentum_decay) * jnp.einsum('mrk,mnk->mrn', ortho_rows, back_rows, precision=peak_magnitude)
    blocked = jnp.abs(residual).reshape(MATS, D, D // BLOCK, BLOCK)
    fresh_block_scales = lax.optimization_barrier(jnp.max(blocked, axis=3))
    new_momentum = (residual / (jnp.repeat(fresh_block_scales, BLOCK, axis=2) + epsilon)).astype(jnp.bfloat16)
    update = jnp.einsum('mrk,mnk->mrn', ortho_rows, basis_full, precision=peak_magnitude) * (D / math.sqrt(RANK))
    new_weight = (weight.astype(jnp.float32) - step_size * update).astype(jnp.bfloat16)
    return (new_momentum, fresh_block_scales, basis_full.astype(jnp.bfloat16), new_weight)
```

```python
import functools
import math

import jax
import jax.numpy as jnp
from jax import lax
from jax.experimental import pallas as pl
from jax.experimental.pallas import tpu as pltpu
from jax.sharding import PartitionSpec as P

BLOCK = 2048
LANES = 128
epsilon = 1e-06
momentum_decay = 0.95
step_size = 0.5
HIGHEST = lax.Precision.HIGHEST
VMEM_LIMIT = 56 * 1024 * 1024


def params(**more):
    return pltpu.CompilerParams(vmem_limit_bytes=VMEM_LIMIT, **more)


def decode_kernel(span, codes_ref, scale_ref, table_ref, grad_ref, basis_ref, hi_ref, power_ref, lo_ref):
    rows, cols = hi_ref.shape[1:]
    sub = min(rows, 64)
    parts = table_ref.shape[0]

    def row_step(i, carry):
        at = pl.ds(pl.multiple_of(i * sub, sub), sub)
        tables = [jnp.broadcast_to(table_ref[p : p + 1, :], (sub, LANES)) for p in range(parts)]
        for c in range(cols // LANES):
            cut = slice(c * LANES, (c + 1) * LANES)
            codes = codes_ref[0, at, cut]
            low = codes % LANES if parts == 1 else lax.bitwise_and(codes, LANES - 1)
            value = jnp.take_along_axis(tables[0], low, axis=1)
            for p in range(1, parts):
                value = jnp.where(codes >= p * LANES, jnp.take_along_axis(tables[p], low, axis=1), value)
            block = (c * LANES) // span
            scale = scale_ref[0, at, block : block + 1]
            whole = value * scale + grad_ref[0, at, cut].astype(jnp.float32)
            hi = whole.astype(jnp.bfloat16)
            hi_ref[0, at, cut] = hi
            lo_ref[at, cut] = (whole - hi.astype(jnp.float32)).astype(jnp.bfloat16)
        return carry

    lax.fori_loop(0, rows // sub, row_step, 0)
    basis = basis_ref[0]
    power_ref[0] = jnp.dot(hi_ref[0], basis, preferred_element_type=jnp.float32) + jnp.dot(
        lo_ref[...], basis, preferred_element_type=jnp.float32
    )


def decode_power(codes, scales, table, gradient, basis):
    mats, rows, cols = codes.shape
    rank = basis.shape[2]
    tile = min(rows, 256)
    blocks = scales.shape[2]
    span = cols // blocks
    halves = table.reshape(-1, LANES)
    return pl.pallas_call(
        functools.partial(decode_kernel, span),
        grid=(mats, rows // tile),
        in_specs=[
            pl.BlockSpec((1, tile, cols), lambda m, i: (m, i, 0)),
            pl.BlockSpec((1, tile, blocks), lambda m, i: (m, i, 0)),
            pl.BlockSpec(halves.shape, lambda m, i: (0, 0)),
            pl.BlockSpec((1, tile, cols), lambda m, i: (m, i, 0)),
            pl.BlockSpec((1, cols, rank), lambda m, i: (m, 0, 0)),
        ],
        out_specs=[
            pl.BlockSpec((1, tile, cols), lambda m, i: (m, i, 0)),
            pl.BlockSpec((1, tile, rank), lambda m, i: (m, i, 0)),
        ],
        out_shape=[
            jax.ShapeDtypeStruct((mats, rows, cols), jnp.bfloat16),
            jax.ShapeDtypeStruct((mats, rows, rank), jnp.float32),
        ],
        scratch_shapes=[pltpu.VMEM((tile, cols), jnp.bfloat16)],
        compiler_params=params(),
        cost_estimate=pl.CostEstimate(flops=4 * mats * rows * cols * rank, bytes_accessed=8 * mats * rows * cols, transcendentals=0),
    )(codes, scales, halves, gradient, basis)


def gram_of(rows_block):
    return lax.dot_general(
        rows_block, rows_block, (((0,), (0,)), ((), ())), precision=HIGHEST, preferred_element_type=jnp.float32
    )


def gram_kernel(power_ref, gram_ref):
    gram_ref[0] = gram_of(power_ref[0])


def gram_local(power):
    mats, rows, rank = power.shape
    return pl.pallas_call(
        gram_kernel,
        grid=(mats,),
        in_specs=[pl.BlockSpec((1, rows, rank), lambda m: (m, 0, 0))],
        out_specs=pl.BlockSpec((1, rank, rank), lambda m: (m, 0, 0)),
        out_shape=jax.ShapeDtypeStruct((mats, rank, rank), jnp.float32),
        compiler_params=params(),
    )(power)


def cross_kernel(power_ref, hi_ref, cross_ref, turned_ref):
    @pl.when(pl.program_id(1) == 0)
    def _():
        turned_ref[...] = power_ref[0].T.astype(jnp.bfloat16)

    cross_ref[0] = jnp.dot(turned_ref[...], hi_ref[0], preferred_element_type=jnp.float32)


def cross_local(power, hi):
    mats, rows, cols = hi.shape
    rank = power.shape[2]
    tile = min(cols, 1024)
    return pl.pallas_call(
        cross_kernel,
        grid=(mats, cols // tile),
        in_specs=[
            pl.BlockSpec((1, rows, rank), lambda m, j: (m, 0, 0)),
            pl.BlockSpec((1, rows, tile), lambda m, j: (m, 0, j)),
        ],
        out_specs=pl.BlockSpec((1, rank, tile), lambda m, j: (m, 0, j)),
        out_shape=jax.ShapeDtypeStruct((mats, rank, cols), jnp.float32),
        scratch_shapes=[pltpu.VMEM((rank, rows), jnp.bfloat16)],
        compiler_params=params(),
    )(power, hi)


def back_kernel(inverse_ref, cross_ref, back_ref, square_ref):
    back = jnp.dot(inverse_ref[0], cross_ref[0], precision=HIGHEST, preferred_element_type=jnp.float32)
    back_ref[0] = back
    squares = jnp.sum(back * back, axis=1, keepdims=True)
    first = pl.program_id(1) == 0

    @pl.when(first)
    def _():
        square_ref[0] = squares

    @pl.when(jnp.logical_not(first))
    def _():
        square_ref[0] += squares


def back_local(inverse, cross):
    mats, rank, cols = cross.shape
    tile = min(cols, 1024)
    return pl.pallas_call(
        back_kernel,
        grid=(mats, cols // tile),
        in_specs=[
            pl.BlockSpec((1, rank, rank), lambda m, j: (m, 0, 0)),
            pl.BlockSpec((1, rank, tile), lambda m, j: (m, 0, j)),
        ],
        out_specs=[
            pl.BlockSpec((1, rank, tile), lambda m, j: (m, 0, j)),
            pl.BlockSpec((1, rank, 1), lambda m, j: (m, 0, 0)),
        ],
        out_shape=[
            jax.ShapeDtypeStruct((mats, rank, cols), jnp.float32),
            jax.ShapeDtypeStruct((mats, rank, 1), jnp.float32),
        ],
        compiler_params=params(),
    )(inverse, cross)


def final_kernel(
    whole_blocks, factor, power_ref, inverse_ref, norm_ref, back_ref, part_ref, hi_ref, weight_ref,
    momentum_ref, peak_ref, basis_ref, weight_out_ref, back16_ref,
):
    @pl.when(pl.program_id(1) == 0)
    def _():
        back16_ref[...] = back_ref[0].astype(jnp.bfloat16)

    tile, cols = hi_ref.shape[1:]
    ortho = lax.dot_general(
        power_ref[0], inverse_ref[0], (((1,), (1,)), ((), ())), precision=HIGHEST, preferred_element_type=jnp.float32
    )
    inv_norm = lax.rsqrt(norm_ref[0] + epsilon)
    left = jnp.concatenate([ortho * (1.0 - momentum_decay), ortho * inv_norm * factor], axis=0).astype(jnp.bfloat16)
    span = min(cols, BLOCK)
    for b in range(cols // span):
        at = slice(b * span, (b + 1) * span)
        both = jnp.dot(left, back16_ref[:, at], preferred_element_type=jnp.float32)
        residual = hi_ref[0, :, at].astype(jnp.float32) - both[:tile]
        peak = jnp.max(jnp.abs(residual), axis=1, keepdims=True)
        peak_ref[0, :, b : b + 1] = peak
        if whole_blocks:
            momentum_ref[0, :, at] = (residual * (1.0 / (peak + epsilon))).astype(momentum_ref.dtype)
        else:
            momentum_ref[0, :, at] = residual.astype(momentum_ref.dtype)
        weight_out_ref[0, :, at] = (weight_ref[0, :, at].astype(jnp.float32) - both[tile:]).astype(jnp.bfloat16)
    basis_ref[0] = (part_ref[0].T * inv_norm).astype(jnp.bfloat16)


def final_local(power, inverse, norms, back, hi, weight, factor):
    mats, rows, cols = hi.shape
    rank = power.shape[2]
    tile = min(rows, 128)
    steps = rows // tile
    part = cols // steps
    span = min(cols, BLOCK)
    whole_blocks = cols % BLOCK == 0
    held = jnp.bfloat16 if whole_blocks else jnp.float32
    return pl.pallas_call(
        functools.partial(final_kernel, whole_blocks, factor),
        grid=(mats, steps),
        in_specs=[
            pl.BlockSpec((1, tile, rank), lambda m, i: (m, i, 0)),
            pl.BlockSpec((1, rank, rank), lambda m, i: (m, 0, 0)),
            pl.BlockSpec((1, 1, rank), lambda m, i: (m, 0, 0)),
            pl.BlockSpec((1, rank, cols), lambda m, i: (m, 0, 0)),
            pl.BlockSpec((1, rank, part), lambda m, i: (m, 0, i)),
            pl.BlockSpec((1, tile, cols), lambda m, i: (m, i, 0)),
            pl.BlockSpec((1, tile, cols), lambda m, i: (m, i, 0)),
        ],
        out_specs=[
            pl.BlockSpec((1, tile, cols), lambda m, i: (m, i, 0)),
            pl.BlockSpec((1, tile, cols // span), lambda m, i: (m, i, 0)),
            pl.BlockSpec((1, part, rank), lambda m, i: (m, i, 0)),
            pl.BlockSpec((1, tile, cols), lambda m, i: (m, i, 0)),
        ],
        out_shape=[
            jax.ShapeDtypeStruct((mats, rows, cols), held),
            jax.ShapeDtypeStruct((mats, rows, cols // span), jnp.float32),
            jax.ShapeDtypeStruct((mats, cols, rank), jnp.bfloat16),
            jax.ShapeDtypeStruct((mats, rows, cols), jnp.bfloat16),
        ],
        scratch_shapes=[pltpu.VMEM((rank, cols), jnp.bfloat16)],
        compiler_params=params(),
    )(power, inverse, norms, back, back, hi, weight)


def spread_peaks(peaks, col_start, cols, blocks):
    starts = (col_start + jnp.arange(peaks.shape[2], dtype=jnp.int32) * min(cols, BLOCK)) // BLOCK
    hit = starts[:, None] == jnp.arange(blocks, dtype=jnp.int32)[None, :]
    return lax.pmax(jnp.max(jnp.where(hit[None, None], peaks[..., None], 0.0), axis=2), "cols")


def per_device(codes, scales, table, gradient, weight, basis):
    mats, rows, cols = codes.shape
    blocks = scales.shape[2]
    total_cols = blocks * BLOCK
    rank = basis.shape[2]
    col_start = lax.axis_index("cols") * cols
    span = min(cols, BLOCK)
    local_blocks = cols // span
    own_scales = lax.dynamic_slice_in_dim(scales, col_start // BLOCK, local_blocks, axis=2)
    hi, partial_power = decode_power(codes, own_scales, table, gradient, basis)
    power = lax.psum(partial_power, "cols")
    gram = lax.psum(gram_local(power), "rows")
    cross = lax.psum(cross_local(power, hi), "rows")
    lower = jnp.linalg.cholesky(gram)
    eye = jnp.broadcast_to(jnp.eye(rank, dtype=jnp.float32), gram.shape)
    inverse = lax.linalg.triangular_solve(lower, eye, left_side=True, lower=True)
    back, squares = back_local(inverse, cross)
    norms = lax.psum(squares, "cols").reshape(mats, 1, rank)
    factor = step_size * total_cols / math.sqrt(rank)
    momentum, peaks, new_basis, new_weight = final_local(power, inverse, norms, back, hi, weight, factor)
    fresh = spread_peaks(peaks, col_start, cols, blocks)
    if cols % BLOCK != 0:
        own = lax.dynamic_slice_in_dim(fresh, col_start // BLOCK, local_blocks, axis=2)
        columns = jnp.broadcast_to(own[..., None], own.shape + (span,)).reshape(mats, rows, cols)
        momentum = (momentum / (columns + epsilon)).astype(jnp.bfloat16)
    return momentum, fresh, new_basis, new_weight


def solution(mesh):
    placed = (
        P(None, "rows", "cols"),
        P(None, "rows", None),
        P(),
        P(None, "rows", "cols"),
        P(None, "rows", "cols"),
        P(None, "cols", None),
    )
    return jax.shard_map(
        per_device,
        mesh=mesh,
        in_specs=placed,
        out_specs=(
            P(None, "rows", "cols"),
            P(None, "rows", None),
            P(None, "cols", None),
            P(None, "rows", "cols"),
        ),
        check_vma=False,
    )
```

```python
import functools
import math

import jax
import jax.numpy as jnp
from jax import lax
from jax.experimental import pallas as pl
from jax.experimental.pallas import tpu as pltpu
from jax.sharding import PartitionSpec as P

BLOCK = 2048
LANES = 128
epsilon = 1e-06
momentum_decay = 0.95
step_size = 0.5
HIGHEST = lax.Precision.HIGHEST
VMEM_LIMIT = 56 * 1024 * 1024


def params(**more):
    return pltpu.CompilerParams(vmem_limit_bytes=VMEM_LIMIT, **more)


def decode_kernel(span, codes_ref, scale_ref, table_ref, grad_ref, basis_ref, hi_ref, power_ref, lo_ref):
    rows, cols = hi_ref.shape[1:]
    sub = min(rows, 64)
    parts = table_ref.shape[0]

    def row_step(i, carry):
        at = pl.ds(pl.multiple_of(i * sub, sub), sub)
        tables = [jnp.broadcast_to(table_ref[p : p + 1, :], (sub, LANES)) for p in range(parts)]
        for c in range(cols // LANES):
            cut = slice(c * LANES, (c + 1) * LANES)
            codes = codes_ref[0, at, cut]
            low = codes % LANES if parts == 1 else lax.bitwise_and(codes, LANES - 1)
            value = jnp.take_along_axis(tables[0], low, axis=1)
            for p in range(1, parts):
                value = jnp.where(codes >= p * LANES, jnp.take_along_axis(tables[p], low, axis=1), value)
            block = (c * LANES) // span
            scale = scale_ref[0, at, block : block + 1]
            whole = value * scale + grad_ref[0, at, cut].astype(jnp.float32)
            hi = whole.astype(jnp.bfloat16)
            hi_ref[0, at, cut] = hi
            lo_ref[at, cut] = (whole - hi.astype(jnp.float32)).astype(jnp.bfloat16)
        return carry

    lax.fori_loop(0, rows // sub, row_step, 0)
    basis = basis_ref[0]
    power_ref[0] = jnp.dot(hi_ref[0], basis, preferred_element_type=jnp.float32) + jnp.dot(
        lo_ref[...], basis, preferred_element_type=jnp.float32
    )


def decode_power(codes, scales, table, gradient, basis):
    mats, rows, cols = codes.shape
    rank = basis.shape[2]
    tile = min(rows, 256)
    blocks = scales.shape[2]
    span = cols // blocks
    halves = table.reshape(-1, LANES)
    return pl.pallas_call(
        functools.partial(decode_kernel, span),
        grid=(mats, rows // tile),
        in_specs=[
            pl.BlockSpec((1, tile, cols), lambda m, i: (m, i, 0)),
            pl.BlockSpec((1, tile, blocks), lambda m, i: (m, i, 0)),
            pl.BlockSpec(halves.shape, lambda m, i: (0, 0)),
            pl.BlockSpec((1, tile, cols), lambda m, i: (m, i, 0)),
            pl.BlockSpec((1, cols, rank), lambda m, i: (m, 0, 0)),
        ],
        out_specs=[
            pl.BlockSpec((1, tile, cols), lambda m, i: (m, i, 0)),
            pl.BlockSpec((1, tile, rank), lambda m, i: (m, i, 0)),
        ],
        out_shape=[
            jax.ShapeDtypeStruct((mats, rows, cols), jnp.bfloat16),
            jax.ShapeDtypeStruct((mats, rows, rank), jnp.float32),
        ],
        scratch_shapes=[pltpu.VMEM((tile, cols), jnp.bfloat16)],
        compiler_params=params(),
        cost_estimate=pl.CostEstimate(flops=4 * mats * rows * cols * rank, bytes_accessed=8 * mats * rows * cols, transcendentals=0),
    )(codes, scales, halves, gradient, basis)


def gram_of(rows_block):
    return lax.dot_general(
        rows_block, rows_block, (((0,), (0,)), ((), ())), precision=HIGHEST, preferred_element_type=jnp.float32
    )


def gram_kernel(power_ref, gram_ref):
    gram_ref[0] = gram_of(power_ref[0])


def gram_local(power):
    mats, rows, rank = power.shape
    return pl.pallas_call(
        gram_kernel,
        grid=(mats,),
        in_specs=[pl.BlockSpec((1, rows, rank), lambda m: (m, 0, 0))],
        out_specs=pl.BlockSpec((1, rank, rank), lambda m: (m, 0, 0)),
        out_shape=jax.ShapeDtypeStruct((mats, rank, rank), jnp.float32),
        compiler_params=params(),
    )(power)


def cross_kernel(power_ref, hi_ref, cross_ref, turned_ref):
    @pl.when(pl.program_id(1) == 0)
    def _():
        turned_ref[...] = power_ref[0].T.astype(jnp.bfloat16)

    cross_ref[0] = jnp.dot(turned_ref[...], hi_ref[0], preferred_element_type=jnp.float32)


def cross_local(power, hi):
    mats, rows, cols = hi.shape
    rank = power.shape[2]
    tile = min(cols, 1024)
    return pl.pallas_call(
        cross_kernel,
        grid=(mats, cols // tile),
        in_specs=[
            pl.BlockSpec((1, rows, rank), lambda m, j: (m, 0, 0)),
            pl.BlockSpec((1, rows, tile), lambda m, j: (m, 0, j)),
        ],
        out_specs=pl.BlockSpec((1, rank, tile), lambda m, j: (m, 0, j)),
        out_shape=jax.ShapeDtypeStruct((mats, rank, cols), jnp.float32),
        scratch_shapes=[pltpu.VMEM((rank, rows), jnp.bfloat16)],
        compiler_params=params(),
    )(power, hi)


def back_kernel(inverse_ref, cross_ref, back_ref, square_ref):
    back = jnp.dot(inverse_ref[0], cross_ref[0], precision=HIGHEST, preferred_element_type=jnp.float32)
    back_ref[0] = back
    squares = jnp.sum(back * back, axis=1, keepdims=True)
    first = pl.program_id(1) == 0

    @pl.when(first)
    def _():
        square_ref[0] = squares

    @pl.when(jnp.logical_not(first))
    def _():
        square_ref[0] += squares


def back_local(inverse, cross):
    mats, rank, cols = cross.shape
    tile = min(cols, 1024)
    return pl.pallas_call(
        back_kernel,
        grid=(mats, cols // tile),
        in_specs=[
            pl.BlockSpec((1, rank, rank), lambda m, j: (m, 0, 0)),
            pl.BlockSpec((1, rank, tile), lambda m, j: (m, 0, j)),
        ],
        out_specs=[
            pl.BlockSpec((1, rank, tile), lambda m, j: (m, 0, j)),
            pl.BlockSpec((1, rank, 1), lambda m, j: (m, 0, 0)),
        ],
        out_shape=[
            jax.ShapeDtypeStruct((mats, rank, cols), jnp.float32),
            jax.ShapeDtypeStruct((mats, rank, 1), jnp.float32),
        ],
        compiler_params=params(),
    )(inverse, cross)


def final_kernel(
    whole_blocks, factor, power_ref, inverse_ref, norm_ref, back_ref, part_ref, hi_ref, weight_ref,
    momentum_ref, peak_ref, basis_ref, weight_out_ref, back16_ref,
):
    @pl.when(pl.program_id(1) == 0)
    def _():
        back16_ref[...] = back_ref[0].astype(jnp.bfloat16)

    tile, cols = hi_ref.shape[1:]
    ortho = lax.dot_general(
        power_ref[0], inverse_ref[0], (((1,), (1,)), ((), ())), precision=HIGHEST, preferred_element_type=jnp.float32
    )
    inv_norm = lax.rsqrt(norm_ref[0] + epsilon)
    left = jnp.concatenate([ortho * (1.0 - momentum_decay), ortho * inv_norm * factor], axis=0).astype(jnp.bfloat16)
    span = min(cols, BLOCK)
    for b in range(cols // span):
        at = slice(b * span, (b + 1) * span)
        both = jnp.dot(left, back16_ref[:, at], preferred_element_type=jnp.float32)
        residual = hi_ref[0, :, at].astype(jnp.float32) - both[:tile]
        peak = jnp.max(jnp.abs(residual), axis=1, keepdims=True)
        peak_ref[0, :, b : b + 1] = peak
        if whole_blocks:
            momentum_ref[0, :, at] = (residual * (1.0 / (peak + epsilon))).astype(momentum_ref.dtype)
        else:
            momentum_ref[0, :, at] = residual.astype(momentum_ref.dtype)
        weight_out_ref[0, :, at] = (weight_ref[0, :, at].astype(jnp.float32) - both[tile:]).astype(jnp.bfloat16)
    basis_ref[0] = (part_ref[0].T * inv_norm).astype(jnp.bfloat16)


def final_local(power, inverse, norms, back, hi, weight, factor):
    mats, rows, cols = hi.shape
    rank = power.shape[2]
    tile = min(rows, 128)
    steps = rows // tile
    part = cols // steps
    span = min(cols, BLOCK)
    whole_blocks = cols % BLOCK == 0
    held = jnp.bfloat16 if whole_blocks else jnp.float32
    return pl.pallas_call(
        functools.partial(final_kernel, whole_blocks, factor),
        grid=(mats, steps),
        in_specs=[
            pl.BlockSpec((1, tile, rank), lambda m, i: (m, i, 0)),
            pl.BlockSpec((1, rank, rank), lambda m, i: (m, 0, 0)),
            pl.BlockSpec((1, 1, rank), lambda m, i: (m, 0, 0)),
            pl.BlockSpec((1, rank, cols), lambda m, i: (m, 0, 0)),
            pl.BlockSpec((1, rank, part), lambda m, i: (m, 0, i)),
            pl.BlockSpec((1, tile, cols), lambda m, i: (m, i, 0)),
            pl.BlockSpec((1, tile, cols), lambda m, i: (m, i, 0)),
        ],
        out_specs=[
            pl.BlockSpec((1, tile, cols), lambda m, i: (m, i, 0)),
            pl.BlockSpec((1, tile, cols // span), lambda m, i: (m, i, 0)),
            pl.BlockSpec((1, part, rank), lambda m, i: (m, i, 0)),
            pl.BlockSpec((1, tile, cols), lambda m, i: (m, i, 0)),
        ],
        out_shape=[
            jax.ShapeDtypeStruct((mats, rows, cols), held),
            jax.ShapeDtypeStruct((mats, rows, cols // span), jnp.float32),
            jax.ShapeDtypeStruct((mats, cols, rank), jnp.bfloat16),
            jax.ShapeDtypeStruct((mats, rows, cols), jnp.bfloat16),
        ],
        scratch_shapes=[pltpu.VMEM((rank, cols), jnp.bfloat16)],
        compiler_params=params(),
    )(power, inverse, norms, back, back, hi, weight)


def spread_peaks(peaks, col_start, cols, blocks):
    starts = (col_start + jnp.arange(peaks.shape[2], dtype=jnp.int32) * min(cols, BLOCK)) // BLOCK
    hit = starts[:, None] == jnp.arange(blocks, dtype=jnp.int32)[None, :]
    return lax.pmax(jnp.max(jnp.where(hit[None, None], peaks[..., None], 0.0), axis=2), "cols")


def factor_kernel(gram_ref, out_ref, left_ref, right_ref):
    mats, rank = gram_ref.shape[:2]
    side = left_ref.shape[1]
    rows = lax.broadcasted_iota(jnp.int32, (side, side), 0)
    lanes = lax.broadcasted_iota(jnp.int32, (side, side), 1)
    full = lambda a, b: lax.dot_general(
        a, b, (((1,), (0,)), ((), ())), precision=HIGHEST, preferred_element_type=jnp.float32
    )
    trail = [gram_ref[m] for m in range(mats)]
    wide_rows = lax.broadcasted_iota(jnp.int32, (rank, rank), 0)
    wide_lanes = lax.broadcasted_iota(jnp.int32, (rank, rank), 1)
    grown = [(wide_rows == wide_lanes).astype(jnp.float32) for _ in range(mats)]
    for b in range(rank // side):
        at = slice(b * side, (b + 1) * side)
        for m in range(mats):
            left_ref[m] = trail[m][at, at]
            right_ref[m] = (rows == lanes).astype(jnp.float32)

        def step(j, carry):
            for m in range(mats):
                left = left_ref[m]
                column = jnp.sum(jnp.where(lanes == j, left, 0.0), axis=1, keepdims=True)
                row = left_ref[m, pl.ds(j, 1), :]
                pivot = jnp.sum(jnp.where(lanes[:1] == j, row, 0.0), axis=1, keepdims=True)
                ratio = jnp.where(rows[:, :1] > j, column / pivot, 0.0)
                other = right_ref[m, pl.ds(j, 1), :]
                left_ref[m] = left - ratio * row
                right_ref[m] = right_ref[m] - ratio * other
            return carry

        lax.fori_loop(0, side, step, 0)
        for m in range(mats):
            pivots = jnp.sum(jnp.where(rows == lanes, left_ref[m], 0.0), axis=1, keepdims=True)
            block = right_ref[m] * lax.rsqrt(pivots)
            upper = full(block, trail[m][at, :])
            top = full(block, grown[m][at, :])
            out_ref[m, at, :] = top
            if (b + 1) * side < rank:
                lower = jnp.where(wide_rows[:, :side] >= (b + 1) * side, upper.T, 0.0)
                trail[m] = trail[m] - full(lower, upper)
                grown[m] = grown[m] - full(lower, top)


def inverse_factor(gram):
    mats, rank = gram.shape[:2]
    side = min(rank, LANES)
    return pl.pallas_call(
        factor_kernel,
        out_shape=jax.ShapeDtypeStruct(gram.shape, jnp.float32),
        scratch_shapes=[pltpu.VMEM((mats, side, side), jnp.float32), pltpu.VMEM((mats, side, side), jnp.float32)],
        compiler_params=params(),
        cost_estimate=pl.CostEstimate(flops=1500 * mats * rank**3, bytes_accessed=8 * mats * rank * rank, transcendentals=0),
    )(gram)


def swap(value, axis, size, bit):
    return lax.ppermute(value, axis, [(i, i ^ (1 << bit)) for i in range(size)])


def doubled_sum(value, axis):
    size = lax.axis_size(axis)
    if size & (size - 1):
        return lax.psum(value, axis)
    for bit in range(size.bit_length() - 1):
        value = value + swap(value, axis, size, bit)
    return value


def halved_sum(value, axis, early):
    size = lax.axis_size(axis)
    height = value.shape[1]
    if size & (size - 1) or height % size or size < 4:
        return lax.psum(value, axis), early
    cols = value.shape[2]
    first = cols * 3 // 8
    bits = list(range(size.bit_length() - 1))
    turn = len(bits) // 2
    orders = [bits, [bits[1], bits[0]] + bits[2:], bits[turn:] + bits[:turn]]
    parts = [value[:, :, :first], value[:, :, first : 2 * first], value[:, :, 2 * first :]]
    place = lax.axis_index(axis)
    for step in range(len(bits)):
        for p, order in enumerate(orders):
            side = (place >> order[step]) & 1
            half = parts[p].shape[1] // 2
            away = lax.dynamic_slice_in_dim(parts[p], (1 - side) * half, half, axis=1)
            kept = lax.dynamic_slice_in_dim(parts[p], side * half, half, axis=1)
            parts[p] = kept + swap(away, axis, size, order[step])
    *parts, early = lax.optimization_barrier((*parts, early))
    for step in reversed(range(len(bits))):
        for p, order in enumerate(orders):
            upper = ((place >> order[step]) & 1) == 1
            other = swap(parts[p], axis, size, order[step])
            parts[p] = jnp.concatenate(
                [jnp.where(upper, other, parts[p]), jnp.where(upper, parts[p], other)], axis=1
            )
    return jnp.concatenate(parts, axis=2), early


def per_device(codes, scales, table, gradient, weight, basis):
    mats, rows, cols = codes.shape
    blocks = scales.shape[2]
    total_cols = blocks * BLOCK
    rank = basis.shape[2]
    col_start = lax.axis_index("cols") * cols
    span = min(cols, BLOCK)
    local_blocks = cols // span
    own_scales = lax.dynamic_slice_in_dim(scales, col_start // BLOCK, local_blocks, axis=2)
    hi, partial_power = decode_power(codes, own_scales, table, gradient, basis)
    power = doubled_sum(partial_power, "cols")
    gram = doubled_sum(gram_local(power), "rows")
    cross, gram = halved_sum(cross_local(power, hi), "rows", gram)
    inverse = inverse_factor(gram)
    back, squares = back_local(inverse, cross)
    norms = lax.psum(squares, "cols").reshape(mats, 1, rank)
    factor = step_size * total_cols / math.sqrt(rank)
    momentum, peaks, new_basis, new_weight = final_local(power, inverse, norms, back, hi, weight, factor)
    fresh = spread_peaks(peaks, col_start, cols, blocks)
    if cols % BLOCK != 0:
        own = lax.dynamic_slice_in_dim(fresh, col_start // BLOCK, local_blocks, axis=2)
        columns = jnp.broadcast_to(own[..., None], own.shape + (span,)).reshape(mats, rows, cols)
        momentum = (momentum / (columns + epsilon)).astype(jnp.bfloat16)
    return momentum, fresh, new_basis, new_weight


def solution(mesh):
    placed = (
        P(None, "rows", "cols"),
        P(None, "rows", None),
        P(),
        P(None, "rows", "cols"),
        P(None, "rows", "cols"),
        P(None, "cols", None),
    )
    return jax.shard_map(
        per_device,
        mesh=mesh,
        in_specs=placed,
        out_specs=(
            P(None, "rows", "cols"),
            P(None, "rows", None),
            P(None, "cols", None),
            P(None, "rows", "cols"),
        ),
        check_vma=False,
    )
```
